32 devices in a mesh: row: 8 (over z, y), col: 4 (over x, core).
Axes of the slice: x: 2, y: 2, z: 4, core: 2. Of those that a mesh axis runs over, the one named last changes fastest.
Arguments:
- blocks: bfloat16 [16384, 128, 128], P(('row', 'col')), may hold values from -0.046875 to 0.046875
- coords: int32 [16384, 2], P(('row', 'col')), may hold values from 0 to 31, as said below
- counts: int32 [32], P(('row', 'col')), may hold values from 1 to 512, as said below
- start_block: float32 [16384, 64], P(('row', 'col')), may hold values from -12 to 12, as said below
Outputs:
- lanczos_basis: float32 [16384, 64], P(('row', 'col'))
- diag_blocks: float32 [2, 64, 64], replicated
- upper_blocks: float32 [2, 64, 64], replicated
The draws below stay inside these ranges and needn't reach their ends.
Inputs may be any that keep to these rules, and one draw needn't show every extreme that they name: `coords`: within one device's 512 slots the coordinate pairs are distinct; block rows lie below 16 and block columns below 32. `counts`: slot s of a device is live exactly when s is below the device's count; some device has all 512 slots live in every draw. `start_block`: finite values of order one.
All inputs are finite; a program needn't handle non-finite values.
Results may differ from the reference program's by a relative error of at most 0.0049.
Values may be sent and summed in bfloat16 or wider, within the bound.
A program may use at most 128 MiB of HBM per device.

```python
import jax
import jax.numpy as jnp
from jax import lax

BS = 128
K = 64
ITERS = 2
SLOTS = 512
N = 16384
PIECE_BLOCKS = 4
ROW_BLOCKS = 16
COL_BLOCKS = 32
N_ROW = 8
N_COL = 4


def draw_coords(key, part):
    device_total = N_ROW * N_COL
    positions = ROW_BLOCKS * COL_BLOCKS

    def one_device(device):
        order = jax.random.permutation(jax.random.fold_in(key, device), positions)[:SLOTS]
        return jnp.stack([order // COL_BLOCKS, order % COL_BLOCKS], axis=1).astype(jnp.int32)
    table = jax.vmap(one_device)(jnp.arange(device_total, dtype=jnp.int32))
    return table.reshape(device_total * SLOTS, 2)


def draw_counts(key, part):
    device_total = N_ROW * N_COL
    floor_count = max(1, SLOTS // 16)
    first_key = jax.random.fold_in(key, 11)
    second_key = jax.random.fold_in(key, 12)
    level = jax.random.randint(first_key, (device_total,), 0, 32)
    loads = floor_count + (SLOTS - floor_count) * level * level // 961
    busiest = jax.random.randint(second_key, (), 0, device_total)
    loads = loads.at[busiest].set(SLOTS)
    return loads.astype(jnp.int32)


def draw_start_block(key, part):
    position = jnp.arange(N, dtype=jnp.float32)[:, None] / N
    values = jnp.clip(jax.random.normal(key, (N, K), jnp.float32), -6.0, 6.0) * (1.0 + position)
    return values.astype(jnp.float32)


def shard_levels(stream_key, shape, cuts, least, largest):
    factor_of = 1.0
    for axis_at, parts in cuts:
        heights = jax.random.uniform(jax.random.fold_in(jax.random.fold_in(stream_key, 6), axis_at), (parts,), jnp.float32, least / len(cuts), largest / len(cuts))
        factor_of = factor_of * jnp.repeat(jnp.exp(heights), shape[axis_at] // parts).reshape((-1,) + (1,) * (len(shape) - 1 - axis_at))
    return factor_of


def normal_values(key, dims, spread, most, split=(), kind=jnp.bfloat16):
    drawn = jax.random.normal(key, dims, jnp.float32) * spread
    if len(split) > 0:
        drawn = shard_levels(key, dims, split, -0.22, 0.18) * drawn
    return jnp.clip(drawn, min=-most, max=most).astype(kind)


def setup_inputs(seed: int = 0) -> dict:
    key_list = jax.random.split(jax.random.key(seed), 5)
    blocks = normal_values(key_list[0], (N_ROW * N_COL * SLOTS, BS, BS), (BS * SLOTS // 4) ** -0.5, 0.046875, ((0, 32),))
    coords = draw_coords(jax.random.fold_in(key_list[4], 71), 0)
    counts = draw_counts(jax.random.fold_in(key_list[4], 71), 0)
    start_block = draw_start_block(jax.random.fold_in(key_list[4], 71), 0)
    return {"blocks": blocks, "coords": coords, "counts": counts, "start_block": start_block}


def orthonormal(panel, gram_now):
    lower = jnp.linalg.cholesky(gram_now)
    inverse = jax.scipy.linalg.solve_triangular(lower, jnp.eye(gram_now.shape[0], dtype=jnp.float32), lower=True)
    return (jnp.dot(panel, inverse.T, precision=lax.Precision.HIGHEST), lower.T)

def apply_matrix(packed, slabs, pairs, counts):
    tiles = packed.reshape(N // BS, BS, K)
    device_ids = jnp.arange(N_ROW * N_COL, dtype=jnp.int32)

    def visit(total, item):
        slab, pair, live_count, device = item
        row_group = device // N_COL
        col_group = device % N_COL
        global_row = (row_group * ROW_BLOCKS + pair[:, 0]).astype(jnp.int32)
        global_col = ((pair[:, 1] // PIECE_BLOCKS * N_COL + col_group) * PIECE_BLOCKS + pair[:, 1] % PIECE_BLOCKS).astype(jnp.int32)
        live_mask = (jnp.arange(SLOTS, dtype=jnp.int32) < live_count).astype(jnp.float32)[:, None, None]
        slab_wide = slab.astype(jnp.float32)
        forward = jnp.einsum('sij,sjk->sik', slab_wide, tiles[global_col].astype(jnp.float32), precision=lax.Precision.HIGHEST) * live_mask
        backward = jnp.einsum('sij,sik->sjk', slab_wide, tiles[global_row].astype(jnp.float32), precision=lax.Precision.HIGHEST) * live_mask
        total = total.at[global_row].add(forward)
        total = total.at[global_col].add(backward)
        return (total, None)
    start_total = jnp.zeros((N // BS, BS, K), jnp.float32)
    total, unused = lax.scan(visit, start_total, (slabs, pairs, counts, device_ids))
    return total.reshape(N, K)

def reference(blocks, coords, counts, start_block):
    slabs = blocks.reshape(N_ROW * N_COL, SLOTS, BS, BS)
    pairs = coords.reshape(N_ROW * N_COL, SLOTS, 2)
    high = lax.Precision.HIGHEST
    first_gram = jnp.dot(start_block.T, start_block, precision=high) / N
    current, unused = orthonormal(start_block, first_gram)
    previous = jnp.zeros_like(current)
    diagonal_list = []
    upper_list = []
    for iteration in range(ITERS):
        packed = current.astype(jnp.bfloat16)
        applied = current + apply_matrix(packed, slabs, pairs, counts)
        along_now = jnp.dot(current.T, applied, precision=high) / N
        along_prev = jnp.dot(previous.T, applied, precision=high) / N
        residual = applied - jnp.dot(current, along_now, precision=high) - jnp.dot(previous, along_prev, precision=high)
        resid_gram = jnp.dot(residual.T, residual, precision=high) / N
        next_basis, upper = orthonormal(residual, resid_gram)
        diagonal_list.append(along_now)
        upper_list.append(upper)
        previous, current = (current, next_basis)
    return (current, jnp.stack(diagonal_list), jnp.stack(upper_list))
```

```python
import functools

import jax
import jax.numpy as jnp
from jax import lax
from jax.experimental import pallas as pl
from jax.experimental.pallas import tpu as pltpu
from jax.sharding import PartitionSpec as P

ITERS = 2
MESH = pl.DeviceIdType.MESH
HIGH = lax.Precision.HIGHEST
NT = (((1,), (1,)), ((), ()))


def factor(gram2, width):
    row_id = lax.broadcasted_iota(jnp.int32, gram2.shape, 0)
    lane_id = lax.broadcasted_iota(jnp.int32, gram2.shape, 1)
    eye = jnp.where(lane_id - width == row_id, 1.0, 0.0)
    start = jnp.where(lane_id < width, gram2, eye)

    def step(k, now):
        row = jnp.sum(jnp.where(row_id == k, now, 0.0), axis=0, keepdims=True)
        column = jnp.sum(jnp.where(lane_id == k, now, 0.0), axis=1, keepdims=True)
        pivot = jnp.sum(jnp.where(row_id[:, :1] == k, column, 0.0), axis=0, keepdims=True)
        scale = jnp.where(row_id[:, :1] > k, column / pivot, 0.0)
        return now - scale * row

    done = lax.fori_loop(0, width, step, start)
    pivots = jnp.sum(jnp.where(lane_id == row_id, done, 0.0), axis=1, keepdims=True)
    done = done * (1.0 / jnp.sqrt(pivots))
    return jnp.where((lane_id >= width) | (lane_id >= row_id), done, 0.0)


def kernel(
    n_row, n_col, piece_blocks, total_rows,
    table_ref, blocks_hbm, start_ref,
    basis_ref, diag_ref, upper_ref,
    blocks_v, panels, row_x, col_x, row_out, col_out, row_in, col_in, row_own, col_own,
    ar_src, ar_one, ar_two, ar_three,
    load_sem, s_rx, r_rx, s_cx, r_cx, s_ro, r_ro, s_co, r_co, s_a1, r_a1, s_a2, r_a2, s_a3, r_a3,
):
    r = lax.axis_index("row")
    c = lax.axis_index("col")
    slots = blocks_hbm.shape[0]
    bs = blocks_hbm.shape[1]
    width, rows_dev = start_ref.shape
    col_blocks = n_row * piece_blocks

    load = pltpu.make_async_copy(blocks_hbm, blocks_v.at[pl.ds(0, slots)], load_sem)
    load.start()
    blocks_v[slots] = jnp.zeros((bs, bs), jnp.bfloat16)

    barrier = pltpu.get_barrier_semaphore()
    for axis, n, me in (("row", n_row, r), ("col", n_col, c)):

        def greet(k, carry, axis=axis, n=n, me=me):
            pl.semaphore_signal(
                barrier, inc=1, device_id={axis: lax.rem(me + k, n)}, device_id_type=MESH
            )
            return carry

        lax.fori_loop(1, n, greet, 0)
    pl.semaphore_wait(barrier, n_row + n_col - 2)

    def peers(axis, action):
        n, me = (n_row, r) if axis == "row" else (n_col, c)

        def body(k, carry):
            action(lax.rem(me + k, n))
            return carry

        lax.fori_loop(1, n, body, 0)

    def copy(axis, peer, src, dst, send, recv):
        return pltpu.make_async_remote_copy(
            src_ref=src, dst_ref=dst, send_sem=send, recv_sem=recv,
            device_id={axis: peer}, device_id_type=MESH,
        )

    def exchange(axis, slot, src_of, into, send, recv):
        me = r if axis == "row" else c

        def go(p):
            copy(axis, p, src_of(p), into.at[slot, me], send.at[slot, p], recv.at[slot, me]).start()

        peers(axis, go)

    def arrived(axis, slot, p, src, into, send, recv):
        copy(axis, p, src, into.at[slot, p], send.at[slot, p], recv.at[slot, p]).wait_recv()

    def sent(axis, slot, src_of, into, send, recv):
        peers(
            axis,
            lambda p: copy(
                axis, p, src_of(p), into.at[slot, p], send.at[slot, p], recv.at[slot, p]
            ).wait_send(),
        )

    def settle(axis, slot, src_of, into, send, recv):
        peers(axis, lambda p: arrived(axis, slot, p, src_of(p), into, send, recv))
        sent(axis, slot, src_of, into, send, recv)

    def add_up(into, slot, n):
        return functools.reduce(jnp.add, [into[slot, i] for i in range(n)])

    def all_reduce(slot, value):
        ar_src[slot] = value.reshape(ar_src.shape[1:])
        src = lambda p: ar_src.at[slot, p]
        exchange("col", slot, src, ar_one, s_a1, r_a1)
        ar_one[slot, c] = ar_src[slot, c]
        settle("col", slot, src, ar_one, s_a1, r_a1)
        ar_two[slot, r] = add_up(ar_one, slot, n_col)
        src = lambda p: ar_two.at[slot, r]
        exchange("row", slot, src, ar_two, s_a2, r_a2)
        settle("row", slot, src, ar_two, s_a2, r_a2)
        ar_three[slot, c] = add_up(ar_two, slot, n_row)
        src = lambda p: ar_three.at[slot, c]
        exchange("col", slot, src, ar_three, s_a3, r_a3)
        settle("col", slot, src, ar_three, s_a3, r_a3)
        return ar_three[slot].reshape(width, 2 * width)

    def gram_of(panel):
        return lax.dot_general(
            panel, jnp.concatenate([panel, panel], axis=0), NT,
            precision=HIGH, preferred_element_type=jnp.float32,
        )

    def solved(rows, panel):
        both = jnp.concatenate([jnp.zeros_like(panel), panel], axis=0)
        return jnp.dot(rows, both, precision=HIGH, preferred_element_type=jnp.float32)

    first = start_ref[...]
    rows = factor(all_reduce(0, gram_of(first)) / total_rows, width)
    panels[0] = jnp.zeros_like(first)
    panels[1] = solved(rows, first)
    load.wait()

    def block(a, b):
        return blocks_v[table_ref[a * col_blocks + b]]

    def tile(a, rows_of, b, cols_of):
        return jnp.concatenate(
            [
                jnp.concatenate([block(a + i, b + j) for j in range(cols_of)], axis=1)
                for i in range(rows_of)
            ],
            axis=0,
        )

    half = piece_blocks // 2

    def iterate(it, carry):
        current = panels[it + 1]
        packed = current.astype(jnp.bfloat16)
        row_x[it, c] = packed
        col_x[it, r] = packed
        src_rx = lambda p: row_x.at[it, c]
        src_cx = lambda p: col_x.at[it, r]
        exchange("col", it, src_rx, row_x, s_rx, r_rx)
        exchange("row", it, src_cx, col_x, s_cx, r_cx)
        settle("col", it, src_rx, row_x, s_rx, r_rx)

        def backward(k, carry):
            p = lax.rem(r + k, n_row)
            for h in range(2):
                total = jnp.zeros((width, half * bs), jnp.float32)
                for q in range(n_col):
                    total += jnp.dot(
                        row_x[it, q],
                        tile(q * piece_blocks, piece_blocks, p * piece_blocks + h * half, half),
                        preferred_element_type=jnp.float32,
                    )
                at = pl.ds(h * half * bs, half * bs)
                col_own[:, at] = total
                col_out[p, :, at] = total.astype(jnp.bfloat16)

            @pl.when(k < n_row)
            def _():
                copy(
                    "row", p, col_out.at[p], col_in.at[it, r], s_co.at[it, p], r_co.at[it, r]
                ).start()

            return carry

        lax.fori_loop(1, n_row + 1, backward, 0)
        settle("row", it, src_cx, col_x, s_cx, r_cx)

        def forward(k, carry):
            q = lax.rem(c + k, n_col)

            def add_piece(p, totals):
                piece = col_x[it, p]
                return tuple(
                    totals[h]
                    + lax.dot_general(
                        piece,
                        tile(q * piece_blocks + h * half, half, p * piece_blocks, piece_blocks),
                        NT,
                        preferred_element_type=jnp.float32,
                    )
                    for h in range(2)
                )

            zero = jnp.zeros((width, half * bs), jnp.float32)
            totals = lax.fori_loop(0, n_row, add_piece, (zero, zero))
            for h in range(2):
                at = pl.ds(h * half * bs, half * bs)
                row_own[:, at] = totals[h]
                row_out[q, :, at] = totals[h].astype(jnp.bfloat16)

            @pl.when(k < n_col)
            def _():
                copy(
                    "col", q, row_out.at[q], row_in.at[it, c], s_ro.at[it, q], r_ro.at[it, c]
                ).start()

            return carry

        lax.fori_loop(1, n_col + 1, forward, 0)
        col_own[...] += current + row_own[...]

        def take_col(p):
            arrived("row", it, p, col_out.at[p], col_in, s_co, r_co)
            col_own[...] += col_in[it, p].astype(jnp.float32)

        def take_row(p):
            arrived("col", it, p, row_out.at[p], row_in, s_ro, r_ro)
            col_own[...] += row_in[it, p].astype(jnp.float32)

        peers("row", take_col)
        peers("col", take_row)
        sent("row", it, lambda p: col_out.at[p], col_in, s_co, r_co)
        sent("col", it, lambda p: row_out.at[p], row_in, s_ro, r_ro)

        applied = col_own[...]
        pair = jnp.concatenate([current, panels[it]], axis=0)
        along = lax.dot_general(
            applied, pair, NT, precision=HIGH, preferred_element_type=jnp.float32
        )
        along = all_reduce(1 + 2 * it, along) / total_rows
        diag_ref[it] = along
        residual = applied - jnp.dot(
            along, pair, precision=HIGH, preferred_element_type=jnp.float32
        )
        rows = factor(all_reduce(2 + 2 * it, gram_of(residual)) / total_rows, width)
        upper_ref[it] = rows
        panels[it + 2] = solved(rows, residual)
        return carry

    lax.fori_loop(0, ITERS, iterate, 0)
    basis_ref[...] = panels[ITERS + 1]


def per_device(blocks, coords, counts, start_block):
    rows_dev, width = start_block.shape
    slots, bs, _ = blocks.shape
    n_row = lax.axis_size("row")
    n_col = lax.axis_size("col")
    piece_blocks = rows_dev // bs
    row_blocks = n_col * piece_blocks
    col_blocks = n_row * piece_blocks
    slot_ids = jnp.arange(slots, dtype=jnp.int32)
    place = coords[:, 0] * col_blocks + coords[:, 1]
    places = jnp.arange(row_blocks * col_blocks, dtype=jnp.int32)
    hit = (places[:, None] == place[None, :]) & (slot_ids < counts[0])[None, :]
    table = jnp.min(jnp.where(hit, slot_ids[None, :], slots), axis=1)

    quarter = width // n_col
    sums = 1 + 2 * ITERS
    dma = pltpu.SemaphoreType.DMA
    bf16, f32 = jnp.bfloat16, jnp.float32
    vmem = pl.BlockSpec(memory_space=pltpu.VMEM)
    basis, diag, upper = pl.pallas_call(
        functools.partial(
            kernel, n_row, n_col, piece_blocks, float(rows_dev * n_row * n_col)
        ),
        out_shape=(
            jax.ShapeDtypeStruct((width, rows_dev), f32),
            jax.ShapeDtypeStruct((ITERS, width, 2 * width), f32),
            jax.ShapeDtypeStruct((ITERS, width, 2 * width), f32),
        ),
        in_specs=[
            pl.BlockSpec(memory_space=pltpu.SMEM),
            pl.BlockSpec(memory_space=pl.ANY),
            vmem,
        ],
        out_specs=(vmem, vmem, vmem),
        scratch_shapes=[
            pltpu.VMEM((slots + 1, bs, bs), bf16),
            pltpu.VMEM((ITERS + 2, width, rows_dev), f32),
            pltpu.VMEM((ITERS, n_col, width, rows_dev), bf16),
            pltpu.VMEM((ITERS, n_row, width, rows_dev), bf16),
            pltpu.VMEM((n_col, width, rows_dev), bf16),
            pltpu.VMEM((n_row, width, rows_dev), bf16),
            pltpu.VMEM((ITERS, n_col, width, rows_dev), bf16),
            pltpu.VMEM((ITERS, n_row, width, rows_dev), bf16),
            pltpu.VMEM((width, rows_dev), f32),
            pltpu.VMEM((width, rows_dev), f32),
            pltpu.VMEM((sums, n_col, quarter, 2 * width), f32),
            pltpu.VMEM((sums, n_col, quarter, 2 * width), f32),
            pltpu.VMEM((sums, n_row, quarter, 2 * width), f32),
            pltpu.VMEM((sums, n_col, quarter, 2 * width), f32),
            dma,
            dma((ITERS, n_col)), dma((ITERS, n_col)),
            dma((ITERS, n_row)), dma((ITERS, n_row)),
            dma((ITERS, n_col)), dma((ITERS, n_col)),
            dma((ITERS, n_row)), dma((ITERS, n_row)),
            dma((sums, n_col)), dma((sums, n_col)),
            dma((sums, n_row)), dma((sums, n_row)),
            dma((sums, n_col)), dma((sums, n_col)),
        ],
        compiler_params=pltpu.CompilerParams(
            collective_id=0, has_side_effects=True, vmem_limit_bytes=48 * 1024 * 1024
        ),
    )(table, blocks, start_block.T)
    return (
        basis.T,
        jnp.swapaxes(diag[:, :, :width], 1, 2),
        upper[:, :, :width],
    )


def solution(mesh):
    return jax.shard_map(
        per_device,
        mesh=mesh,
        in_specs=(
            P(("row", "col"), None, None),
            P(("row", "col"), None),
            P(("row", "col")),
            P(("row", "col"), None),
        ),
        out_specs=(P(("row", "col"), None), P(), P()),
        check_vma=False,
    )
```

```python
import functools

import jax
import jax.numpy as jnp
from jax import lax
from jax.experimental import pallas as pl
from jax.experimental.pallas import tpu as pltpu
from jax.sharding import PartitionSpec as P

ITERS = 2
MESH = pl.DeviceIdType.MESH
HIGH = lax.Precision.HIGHEST
NT = (((1,), (1,)), ((), ()))
GROUP = 4


def factor(gram2, width):
    row_id = lax.broadcasted_iota(jnp.int32, gram2.shape, 0)
    lane_id = lax.broadcasted_iota(jnp.int32, gram2.shape, 1)
    eye = jnp.where(lane_id - width == row_id, 1.0, 0.0)
    now = jnp.where(lane_id < width, gram2, eye)
    for k in range(0, width, GROUP):
        columns = [
            jnp.broadcast_to(now[:, k + j : k + j + 1], now.shape) for j in range(GROUP)
        ]
        rows = [now[k + j : k + j + 1, :] for j in range(GROUP)]
        scaled = []
        for j in range(GROUP):
            inverse = 1.0 / columns[j][k + j : k + j + 1, :]
            for i in range(j + 1, GROUP):
                ratio = columns[j][k + i : k + i + 1, :] * inverse
                rows[i] = rows[i] - ratio * rows[j]
                columns[i] = columns[i] - ratio * columns[j]
            scaled.append(rows[j] * inverse)
        update = functools.reduce(jnp.add, [columns[j] * scaled[j] for j in range(GROUP)])
        later = jnp.where(row_id >= k + GROUP, now - update, now)
        for j in range(GROUP):
            later = jnp.where(row_id == k + j, rows[j], later)
        now = later
    pivots = jnp.sum(jnp.where(lane_id == row_id, now, 0.0), axis=1, keepdims=True)
    now = now * (1.0 / jnp.sqrt(pivots))
    return jnp.where((lane_id >= width) | (lane_id >= row_id), now, 0.0)


def kernel(
    n_row, n_col, piece_blocks, total_rows,
    table_ref, blocks_hbm, start_ref,
    basis_ref, diag_ref, upper_ref,
    blocks_v, panels, row_x, col_x, row_out, col_out, row_in, col_in, row_own, col_own,
    ar_src, ar_one, ar_two, ar_three,
    load_sem, s_rx, r_rx, s_cx, r_cx, s_ro, r_ro, s_co, r_co, s_a1, r_a1, s_a2, r_a2, s_a3, r_a3,
):
    r = lax.axis_index("row")
    c = lax.axis_index("col")
    slots = blocks_hbm.shape[0]
    bs = blocks_hbm.shape[1]
    width, rows_dev = start_ref.shape
    col_blocks = n_row * piece_blocks

    load = pltpu.make_async_copy(blocks_hbm, blocks_v.at[pl.ds(0, slots)], load_sem)
    load.start()
    blocks_v[slots] = jnp.zeros((bs, bs), jnp.bfloat16)

    barrier = pltpu.get_barrier_semaphore()
    for axis, n, me in (("row", n_row, r), ("col", n_col, c)):

        def greet(k, carry, axis=axis, n=n, me=me):
            pl.semaphore_signal(
                barrier, inc=1, device_id={axis: lax.rem(me + k, n)}, device_id_type=MESH
            )
            return carry

        lax.fori_loop(1, n, greet, 0)
    pl.semaphore_wait(barrier, n_row + n_col - 2)

    def peers(axis, action):
        n, me = (n_row, r) if axis == "row" else (n_col, c)

        def body(k, carry):
            action(lax.rem(me + k, n))
            return carry

        lax.fori_loop(1, n, body, 0)

    def copy(axis, peer, src, dst, send, recv):
        return pltpu.make_async_remote_copy(
            src_ref=src, dst_ref=dst, send_sem=send, recv_sem=recv,
            device_id={axis: peer}, device_id_type=MESH,
        )

    def exchange(axis, slot, src_of, into, send, recv, rows=slice(None)):
        me = r if axis == "row" else c

        def go(p):
            copy(axis, p, src_of(p), into.at[slot, me, rows], send.at[slot, p], recv.at[slot, me]).start()

        peers(axis, go)

    def arrived(axis, slot, p, src, into, send, recv, rows=slice(None)):
        copy(axis, p, src, into.at[slot, p, rows], send.at[slot, p], recv.at[slot, p]).wait_recv()

    def sent(axis, slot, src_of, into, send, recv, rows=slice(None)):
        peers(
            axis,
            lambda p: copy(
                axis, p, src_of(p), into.at[slot, p, rows], send.at[slot, p], recv.at[slot, p]
            ).wait_send(),
        )

    def settle(axis, slot, src_of, into, send, recv, rows=slice(None)):
        peers(axis, lambda p: arrived(axis, slot, p, src_of(p), into, send, recv, rows))
        sent(axis, slot, src_of, into, send, recv, rows)

    def add_up(into, slot, n, rows):
        return functools.reduce(jnp.add, [into[slot, i, rows] for i in range(n)])

    def all_reduce(slot, value):
        part = value.shape[0] // n_col
        rows = pl.ds(0, part)
        ar_src[slot, :, rows] = value.reshape(n_col, part, 2 * width)
        src = lambda p: ar_src.at[slot, p, rows]
        exchange("col", slot, src, ar_one, s_a1, r_a1, rows)
        ar_one[slot, c, rows] = ar_src[slot, c, rows]
        settle("col", slot, src, ar_one, s_a1, r_a1, rows)
        ar_two[slot, r, rows] = add_up(ar_one, slot, n_col, rows)
        src = lambda p: ar_two.at[slot, r, rows]
        exchange("row", slot, src, ar_two, s_a2, r_a2, rows)
        settle("row", slot, src, ar_two, s_a2, r_a2, rows)
        ar_three[slot, c, rows] = add_up(ar_two, slot, n_row, rows)
        src = lambda p: ar_three.at[slot, c, rows]
        exchange("col", slot, src, ar_three, s_a3, r_a3, rows)
        settle("col", slot, src, ar_three, s_a3, r_a3, rows)
        return ar_three[slot, :, rows].reshape(value.shape)

    def fold(gram2):
        lane_id = lax.broadcasted_iota(jnp.int32, (width // 2, 2 * width), 1)
        return jnp.where(lane_id < width, gram2[: width // 2], gram2[width // 2 :])

    def unfold(folded):
        return jnp.concatenate([folded, pltpu.roll(folded, width, 1)], axis=0)

    def gram_of(panel):
        return lax.dot_general(
            panel, jnp.concatenate([panel, panel], axis=0), NT,
            precision=HIGH, preferred_element_type=jnp.float32,
        )

    def solved(rows, panel):
        both = jnp.concatenate([jnp.zeros_like(panel), panel], axis=0)
        return jnp.dot(rows, both, precision=HIGH, preferred_element_type=jnp.float32)

    first = start_ref[...]
    rows = factor(unfold(all_reduce(0, fold(gram_of(first)))) / total_rows, width)
    panels[0] = jnp.zeros_like(first)
    panels[1] = solved(rows, first)
    load.wait()

    def block(a, b):
        return blocks_v[table_ref[a * col_blocks + b]]

    def tile(a, rows_of, b, cols_of):
        return jnp.concatenate(
            [
                jnp.concatenate([block(a + i, b + j) for j in range(cols_of)], axis=1)
                for i in range(rows_of)
            ],
            axis=0,
        )

    half = piece_blocks // 2

    def iterate(it, carry):
        current = panels[it + 1]
        packed = current.astype(jnp.bfloat16)
        row_x[it, c] = packed
        col_x[it, r] = packed
        src_rx = lambda p: row_x.at[it, c]
        src_cx = lambda p: col_x.at[it, r]
        exchange("col", it, src_rx, row_x, s_rx, r_rx)
        exchange("row", it, src_cx, col_x, s_cx, r_cx)
        settle("col", it, src_rx, row_x, s_rx, r_rx)

        def backward(k, carry):
            p = lax.rem(r + k, n_row)
            for h in range(2):
                total = jnp.zeros((width, half * bs), jnp.float32)
                for q in range(n_col):
                    total += jnp.dot(
                        row_x[it, q],
                        tile(q * piece_blocks, piece_blocks, p * piece_blocks + h * half, half),
                        preferred_element_type=jnp.float32,
                    )
                at = pl.ds(h * half * bs, half * bs)
                col_own[:, at] = total
                col_out[p, :, at] = total.astype(jnp.bfloat16)

            @pl.when(k < n_row)
            def _():
                copy(
                    "row", p, col_out.at[p], col_in.at[it, r], s_co.at[it, p], r_co.at[it, r]
                ).start()

            return carry

        lax.fori_loop(1, n_row + 1, backward, 0)
        settle("row", it, src_cx, col_x, s_cx, r_cx)

        def forward(k, carry):
            q = lax.rem(c + k, n_col)

            def add_piece(p, totals):
                piece = col_x[it, p]
                return tuple(
                    totals[h]
                    + lax.dot_general(
                        piece,
                        tile(q * piece_blocks + h * half, half, p * piece_blocks, piece_blocks),
                        NT,
                        preferred_element_type=jnp.float32,
                    )
                    for h in range(2)
                )

            zero = jnp.zeros((width, half * bs), jnp.float32)
            totals = lax.fori_loop(0, n_row, add_piece, (zero, zero))
            for h in range(2):
                at = pl.ds(h * half * bs, half * bs)
                row_own[:, at] = totals[h]
                row_out[q, :, at] = totals[h].astype(jnp.bfloat16)

            @pl.when(k < n_col)
            def _():
                copy(
                    "col", q, row_out.at[q], row_in.at[it, c], s_ro.at[it, q], r_ro.at[it, c]
                ).start()

            return carry

        lax.fori_loop(1, n_col + 1, forward, 0)
        col_own[...] += row_own[...]

        def take_col(p):
            arrived("row", it, p, col_out.at[p], col_in, s_co, r_co)
            col_own[...] += col_in[it, p].astype(jnp.float32)

        def take_row(p):
            arrived("col", it, p, row_out.at[p], row_in, s_ro, r_ro)
            col_own[...] += row_in[it, p].astype(jnp.float32)

        peers("row", take_col)
        peers("col", take_row)
        sent("row", it, lambda p: col_out.at[p], col_in, s_co, r_co)
        sent("col", it, lambda p: row_out.at[p], row_in, s_ro, r_ro)

        applied = col_own[...]
        pair = jnp.concatenate([current, panels[it]], axis=0)
        along = lax.dot_general(
            applied, pair, NT, precision=HIGH, preferred_element_type=jnp.float32
        )
        sums = all_reduce(1 + it, jnp.concatenate([along, fold(gram_of(applied))], axis=0))
        along = sums[:width] / total_rows
        row_id = lax.broadcasted_iota(jnp.int32, along.shape, 0)
        lane_id = lax.broadcasted_iota(jnp.int32, along.shape, 1)
        diag_ref[it] = along + jnp.where(row_id == lane_id, 1.0, 0.0)
        residual = applied - jnp.dot(
            along, pair, precision=HIGH, preferred_element_type=jnp.float32
        )
        gram = unfold(sums[width:]) / total_rows - gram_of(along)
        rows = factor(gram, width)
        upper_ref[it] = rows
        panels[it + 2] = solved(rows, residual)
        return carry

    lax.fori_loop(0, ITERS, iterate, 0)
    basis_ref[...] = panels[ITERS + 1]


def per_device(blocks, coords, counts, start_block):
    rows_dev, width = start_block.shape
    slots, bs, _ = blocks.shape
    n_row = lax.axis_size("row")
    n_col = lax.axis_size("col")
    piece_blocks = rows_dev // bs
    row_blocks = n_col * piece_blocks
    col_blocks = n_row * piece_blocks
    slot_ids = jnp.arange(slots, dtype=jnp.int32)
    place = coords[:, 0] * col_blocks + coords[:, 1]
    places = jnp.arange(row_blocks * col_blocks, dtype=jnp.int32)
    hit = (places[:, None] == place[None, :]) & (slot_ids < counts[0])[None, :]
    table = jnp.min(jnp.where(hit, slot_ids[None, :], slots), axis=1)

    quarter = (width + width // 2) // n_col
    sums = 1 + ITERS
    dma = pltpu.SemaphoreType.DMA
    bf16, f32 = jnp.bfloat16, jnp.float32
    vmem = pl.BlockSpec(memory_space=pltpu.VMEM)
    basis, diag, upper = pl.pallas_call(
        functools.partial(
            kernel, n_row, n_col, piece_blocks, float(rows_dev * n_row * n_col)
        ),
        out_shape=(
            jax.ShapeDtypeStruct((width, rows_dev), f32),
            jax.ShapeDtypeStruct((ITERS, width, 2 * width), f32),
            jax.ShapeDtypeStruct((ITERS, width, 2 * width), f32),
        ),
        in_specs=[
            pl.BlockSpec(memory_space=pltpu.SMEM),
            pl.BlockSpec(memory_space=pl.ANY),
            vmem,
        ],
        out_specs=(vmem, vmem, vmem),
        scratch_shapes=[
            pltpu.VMEM((slots + 1, bs, bs), bf16),
            pltpu.VMEM((ITERS + 2, width, rows_dev), f32),
            pltpu.VMEM((ITERS, n_col, width, rows_dev), bf16),
            pltpu.VMEM((ITERS, n_row, width, rows_dev), bf16),
            pltpu.VMEM((n_col, width, rows_dev), bf16),
            pltpu.VMEM((n_row, width, rows_dev), bf16),
            pltpu.VMEM((ITERS, n_col, width, rows_dev), bf16),
            pltpu.VMEM((ITERS, n_row, width, rows_dev), bf16),
            pltpu.VMEM((width, rows_dev), f32),
            pltpu.VMEM((width, rows_dev), f32),
            pltpu.VMEM((sums, n_col, quarter, 2 * width), f32),
            pltpu.VMEM((sums, n_col, quarter, 2 * width), f32),
            pltpu.VMEM((sums, n_row, quarter, 2 * width), f32),
            pltpu.VMEM((sums, n_col, quarter, 2 * width), f32),
            dma,
            dma((ITERS, n_col)), dma((ITERS, n_col)),
            dma((ITERS, n_row)), dma((ITERS, n_row)),
            dma((ITERS, n_col)), dma((ITERS, n_col)),
            dma((ITERS, n_row)), dma((ITERS, n_row)),
            dma((sums, n_col)), dma((sums, n_col)),
            dma((sums, n_row)), dma((sums, n_row)),
            dma((sums, n_col)), dma((sums, n_col)),
        ],
        compiler_params=pltpu.CompilerParams(
            collective_id=0, has_side_effects=True, vmem_limit_bytes=48 * 1024 * 1024
        ),
    )(table, blocks, start_block.T)
    return (
        basis.T,
        jnp.swapaxes(diag[:, :, :width], 1, 2),
        upper[:, :, :width],
    )


def solution(mesh):
    return jax.shard_map(
        per_device,
        mesh=mesh,
        in_specs=(
            P(("row", "col"), None, None),
            P(("row", "col"), None),
            P(("row", "col")),
            P(("row", "col"), None),
        ),
        out_specs=(P(("row", "col"), None), P(), P()),
        check_vma=False,
    )
```

```python
import functools

import jax
import jax.numpy as jnp
from jax import lax
from jax.experimental import pallas as pl
from jax.experimental.pallas import tpu as pltpu
from jax.sharding import PartitionSpec as P

ITERS = 2
MESH = pl.DeviceIdType.MESH
HIGH = lax.Precision.HIGHEST
NT = (((1,), (1,)), ((), ()))
GROUP = 8


def factor(gram2, width):
    row_id = lax.broadcasted_iota(jnp.int32, gram2.shape, 0)
    lane_id = lax.broadcasted_iota(jnp.int32, gram2.shape, 1)
    eye = jnp.where(lane_id - width == row_id, 1.0, 0.0)
    now = jnp.where(lane_id < width, gram2, eye)
    for k in range(0, width, GROUP):
        columns = [
            jnp.broadcast_to(now[:, k + j : k + j + 1], now.shape) for j in range(GROUP)
        ]
        rows = [now[k + j : k + j + 1, :] for j in range(GROUP)]
        scaled = []
        for j in range(GROUP):
            inverse = 1.0 / columns[j][k + j : k + j + 1, :]
            for i in range(j + 1, GROUP):
                ratio = columns[j][k + i : k + i + 1, :] * inverse
                rows[i] = rows[i] - ratio * rows[j]
                columns[i] = columns[i] - ratio * columns[j]
            scaled.append(rows[j] * inverse)
        update = functools.reduce(jnp.add, [columns[j] * scaled[j] for j in range(GROUP)])
        later = jnp.where(row_id >= k + GROUP, now - update, now)
        for j in range(GROUP):
            later = jnp.where(row_id == k + j, rows[j], later)
        now = later
    pivots = jnp.sum(jnp.where(lane_id == row_id, now, 0.0), axis=1, keepdims=True)
    now = now * (1.0 / jnp.sqrt(pivots))
    return jnp.where((lane_id >= width) | (lane_id >= row_id), now, 0.0)


def kernel(
    n_row, n_col, piece_blocks, total_rows,
    table_ref, blocks_hbm, start_ref,
    basis_ref, diag_ref, upper_ref,
    blocks_v, panels, row_x, col_x, row_out, col_out, row_in, col_in, row_own, col_own,
    ar_src, ar_one, ar_two, ar_three,
    load_sem, s_rx, r_rx, s_cx, r_cx, s_ro, r_ro, s_co, r_co, s_a1, r_a1, s_a2, r_a2, s_a3, r_a3,
):
    r = lax.axis_index("row")
    c = lax.axis_index("col")
    slots = blocks_hbm.shape[0]
    bs = blocks_hbm.shape[1]
    width, rows_dev = start_ref.shape
    col_blocks = n_row * piece_blocks

    load = pltpu.make_async_copy(blocks_hbm, blocks_v.at[pl.ds(0, slots)], load_sem)
    load.start()
    blocks_v[slots] = jnp.zeros((bs, bs), jnp.bfloat16)

    barrier = pltpu.get_barrier_semaphore()
    for axis, n, me in (("row", n_row, r), ("col", n_col, c)):

        def greet(k, carry, axis=axis, n=n, me=me):
            pl.semaphore_signal(
                barrier, inc=1, device_id={axis: lax.rem(me + k, n)}, device_id_type=MESH
            )
            return carry

        lax.fori_loop(1, n, greet, 0)
    pl.semaphore_wait(barrier, n_row + n_col - 2)

    def peers(axis, action):
        n, me = (n_row, r) if axis == "row" else (n_col, c)

        def body(k, carry):
            action(lax.rem(me + k, n))
            return carry

        lax.fori_loop(1, n, body, 0)

    def twin(p):
        return p + 1 - 2 * lax.rem(p, 2)

    pairs = n_row // 2

    def alike(action):
        def body(k, carry):
            action(lax.rem(r + 2 * k, n_row))
            return carry

        lax.fori_loop(1, pairs, body, 0)

    def copy(axis, peer, src, dst, send, recv):
        return pltpu.make_async_remote_copy(
            src_ref=src, dst_ref=dst, send_sem=send, recv_sem=recv,
            device_id={axis: peer}, device_id_type=MESH,
        )

    def exchange(axis, slot, src_of, into, send, recv, rows=slice(None)):
        me = r if axis == "row" else c

        def go(p):
            copy(axis, p, src_of(p), into.at[slot, me, rows], send.at[slot, p], recv.at[slot, me]).start()

        peers(axis, go)

    def arrived(axis, slot, p, src, into, send, recv, rows=slice(None)):
        copy(axis, p, src, into.at[slot, p, rows], send.at[slot, p], recv.at[slot, p]).wait_recv()

    def sent(axis, slot, src_of, into, send, recv, rows=slice(None)):
        peers(
            axis,
            lambda p: copy(
                axis, p, src_of(p), into.at[slot, p, rows], send.at[slot, p], recv.at[slot, p]
            ).wait_send(),
        )

    def settle(axis, slot, src_of, into, send, recv, rows=slice(None)):
        peers(axis, lambda p: arrived(axis, slot, p, src_of(p), into, send, recv, rows))
        sent(axis, slot, src_of, into, send, recv, rows)

    def add_up(into, slot, n, rows):
        return functools.reduce(jnp.add, [into[slot, i, rows] for i in range(n)])

    def all_reduce(slot, value):
        part = value.shape[0] // n_col
        rows = pl.ds(0, part)
        ar_src[slot, :, rows] = value.reshape(n_col, part, 2 * width)
        src = lambda p: ar_src.at[slot, p, rows]
        exchange("col", slot, src, ar_one, s_a1, r_a1, rows)
        ar_one[slot, c, rows] = ar_src[slot, c, rows]
        settle("col", slot, src, ar_one, s_a1, r_a1, rows)
        ar_two[slot, r, rows] = add_up(ar_one, slot, n_col, rows)
        src = lambda p: ar_two.at[slot, r, rows]
        exchange("row", slot, src, ar_two, s_a2, r_a2, rows)
        settle("row", slot, src, ar_two, s_a2, r_a2, rows)
        ar_three[slot, c, rows] = add_up(ar_two, slot, n_row, rows)
        src = lambda p: ar_three.at[slot, c, rows]
        exchange("col", slot, src, ar_three, s_a3, r_a3, rows)
        settle("col", slot, src, ar_three, s_a3, r_a3, rows)
        return ar_three[slot, :, rows].reshape(value.shape)

    def fold(gram2):
        lane_id = lax.broadcasted_iota(jnp.int32, (width // 2, 2 * width), 1)
        return jnp.where(lane_id < width, gram2[: width // 2], gram2[width // 2 :])

    def unfold(folded):
        return jnp.concatenate([folded, pltpu.roll(folded, width, 1)], axis=0)

    def gram_of(panel):
        return lax.dot_general(
            panel, jnp.concatenate([panel, panel], axis=0), NT,
            precision=HIGH, preferred_element_type=jnp.float32,
        )

    def solved(rows, panel):
        both = jnp.concatenate([jnp.zeros_like(panel), panel], axis=0)
        return jnp.dot(rows, both, precision=HIGH, preferred_element_type=jnp.float32)

    first = start_ref[...]
    rows = factor(unfold(all_reduce(0, fold(gram_of(first)))) / total_rows, width)
    panels[0] = jnp.zeros_like(first)
    panels[1] = solved(rows, first)
    load.wait()

    def block(a, b):
        return blocks_v[table_ref[a * col_blocks + b]]

    def tile(a, rows_of, b, cols_of):
        return jnp.concatenate(
            [
                jnp.concatenate([block(a + i, b + j) for j in range(cols_of)], axis=1)
                for i in range(rows_of)
            ],
            axis=0,
        )

    half = piece_blocks // 2

    def iterate(it, carry):
        current = panels[it + 1]
        packed = current.astype(jnp.bfloat16)
        row_x[it, c] = packed
        col_x[it, r] = packed
        src_rx = lambda p: row_x.at[it, c]

        def give(p, piece):
            at = jnp.where(p == twin(r), twin(piece), p)
            return copy(
                "row", p, col_x.at[it, piece], col_x.at[it, piece],
                s_cx.at[it, at], r_cx.at[it, piece],
            )

        exchange("col", it, src_rx, row_x, s_rx, r_rx)
        alike(lambda p: give(p, r).start())
        give(twin(r), r).start()
        settle("col", it, src_rx, row_x, s_rx, r_rx)

        def to_twin(p):
            at = twin(p)
            return copy(
                "row", twin(r), col_out.at[p], col_in.at[it, at], s_co.at[it, p], r_co.at[it, at]
            )

        def backward(k, carry):
            @pl.when((lax.rem(k, 2) == 1) & (k > 1))
            def _():
                piece = lax.rem(r + n_row + 1 - k, n_row)
                give(twin(r), piece).wait_recv()
                give(twin(r), piece).start()

            base = jnp.where(k < pairs, twin(r), r)
            p = lax.rem(base + 2 * (lax.rem(k, pairs) + 1), n_row)
            for h in range(2):
                total = jnp.zeros((width, half * bs), jnp.float32)
                for q in range(n_col):
                    total += jnp.dot(
                        row_x[it, q],
                        tile(q * piece_blocks, piece_blocks, p * piece_blocks + h * half, half),
                        preferred_element_type=jnp.float32,
                    )
                at = pl.ds(h * half * bs, half * bs)
                col_own[:, at] = total

            @pl.when(k < pairs)
            def _():
                col_out[p] = col_own[...].astype(jnp.bfloat16)
                to_twin(p).start()

            @pl.when(k >= pairs)
            def _():
                to_twin(p).wait_recv()
                col_own[...] += col_in[it, twin(p)].astype(jnp.float32)

            @pl.when((k >= pairs) & (k < n_row - 1))
            def _():
                col_out[p] = col_own[...].astype(jnp.bfloat16)
                copy(
                    "row", p, col_out.at[p], col_in.at[it, r], s_co.at[it, p], r_co.at[it, r]
                ).start()

            return carry

        lax.fori_loop(0, n_row, backward, 0)

        def from_twin(k, carry):
            piece = lax.rem(twin(r) + 2 * k, n_row)
            give(twin(r), piece).wait_recv()
            return carry

        lax.fori_loop(0, pairs, from_twin, 0)
        peers("row", lambda p: give(p, r).wait_send())

        def forward(k, carry):
            q = lax.rem(c + k, n_col)

            def add_piece(p, totals):
                piece = col_x[it, p]
                return tuple(
                    totals[h]
                    + lax.dot_general(
                        piece,
                        tile(q * piece_blocks + h * half, half, p * piece_blocks, piece_blocks),
                        NT,
                        preferred_element_type=jnp.float32,
                    )
                    for h in range(2)
                )

            zero = jnp.zeros((width, half * bs), jnp.float32)
            totals = lax.fori_loop(0, n_row, add_piece, (zero, zero))
            for h in range(2):
                at = pl.ds(h * half * bs, half * bs)
                row_own[:, at] = totals[h]
                row_out[q, :, at] = totals[h].astype(jnp.bfloat16)

            @pl.when(k < n_col)
            def _():
                copy(
                    "col", q, row_out.at[q], row_in.at[it, c], s_ro.at[it, q], r_ro.at[it, c]
                ).start()

            return carry

        lax.fori_loop(1, n_col + 1, forward, 0)
        col_own[...] += row_own[...]

        def take_col(p):
            arrived("row", it, p, col_out.at[p], col_in, s_co, r_co)
            col_own[...] += col_in[it, p].astype(jnp.float32)

        def take_row(p):
            arrived("col", it, p, row_out.at[p], row_in, s_ro, r_ro)
            col_own[...] += row_in[it, p].astype(jnp.float32)

        alike(take_col)
        peers("col", take_row)
        sent("row", it, lambda p: col_out.at[p], col_in, s_co, r_co)
        sent("col", it, lambda p: row_out.at[p], row_in, s_ro, r_ro)

        applied = col_own[...]
        pair = jnp.concatenate([current, panels[it]], axis=0)
        along = lax.dot_general(
            applied, pair, NT, precision=HIGH, preferred_element_type=jnp.float32
        )
        sums = all_reduce(1 + it, jnp.concatenate([along, fold(gram_of(applied))], axis=0))
        along = sums[:width] / total_rows
        row_id = lax.broadcasted_iota(jnp.int32, along.shape, 0)
        lane_id = lax.broadcasted_iota(jnp.int32, along.shape, 1)
        diag_ref[it] = along + jnp.where(row_id == lane_id, 1.0, 0.0)
        residual = applied - jnp.dot(
            along, pair, precision=HIGH, preferred_element_type=jnp.float32
        )
        gram = unfold(sums[width:]) / total_rows - gram_of(along)
        rows = factor(gram, width)
        upper_ref[it] = rows
        panels[it + 2] = solved(rows, residual)
        return carry

    lax.fori_loop(0, ITERS, iterate, 0)
    basis_ref[...] = panels[ITERS + 1]


def per_device(blocks, coords, counts, start_block):
    rows_dev, width = start_block.shape
    slots, bs, _ = blocks.shape
    n_row = lax.axis_size("row")
    n_col = lax.axis_size("col")
    piece_blocks = rows_dev // bs
    row_blocks = n_col * piece_blocks
    col_blocks = n_row * piece_blocks
    slot_ids = jnp.arange(slots, dtype=jnp.int32)
    place = coords[:, 0] * col_blocks + coords[:, 1]
    places = jnp.arange(row_blocks * col_blocks, dtype=jnp.int32)
    hit = (places[:, None] == place[None, :]) & (slot_ids < counts[0])[None, :]
    table = jnp.min(jnp.where(hit, slot_ids[None, :], slots), axis=1)

    quarter = (width + width // 2) // n_col
    sums = 1 + ITERS
    dma = pltpu.SemaphoreType.DMA
    bf16, f32 = jnp.bfloat16, jnp.float32
    vmem = pl.BlockSpec(memory_space=pltpu.VMEM)
    basis, diag, upper = pl.pallas_call(
        functools.partial(
            kernel, n_row, n_col, piece_blocks, float(rows_dev * n_row * n_col)
        ),
        out_shape=(
            jax.ShapeDtypeStruct((width, rows_dev), f32),
            jax.ShapeDtypeStruct((ITERS, width, 2 * width), f32),
            jax.ShapeDtypeStruct((ITERS, width, 2 * width), f32),
        ),
        in_specs=[
            pl.BlockSpec(memory_space=pltpu.SMEM),
            pl.BlockSpec(memory_space=pl.ANY),
            vmem,
        ],
        out_specs=(vmem, vmem, vmem),
        scratch_shapes=[
            pltpu.VMEM((slots + 1, bs, bs), bf16),
            pltpu.VMEM((ITERS + 2, width, rows_dev), f32),
            pltpu.VMEM((ITERS, n_col, width, rows_dev), bf16),
            pltpu.VMEM((ITERS, n_row, width, rows_dev), bf16),
            pltpu.VMEM((n_col, width, rows_dev), bf16),
            pltpu.VMEM((n_row, width, rows_dev), bf16),
            pltpu.VMEM((ITERS, n_col, width, rows_dev), bf16),
            pltpu.VMEM((ITERS, n_row, width, rows_dev), bf16),
            pltpu.VMEM((width, rows_dev), f32),
            pltpu.VMEM((width, rows_dev), f32),
            pltpu.VMEM((sums, n_col, quarter, 2 * width), f32),
            pltpu.VMEM((sums, n_col, quarter, 2 * width), f32),
            pltpu.VMEM((sums, n_row, quarter, 2 * width), f32),
            pltpu.VMEM((sums, n_col, quarter, 2 * width), f32),
            dma,
            dma((ITERS, n_col)), dma((ITERS, n_col)),
            dma((ITERS, n_row)), dma((ITERS, n_row)),
            dma((ITERS, n_col)), dma((ITERS, n_col)),
            dma((ITERS, n_row)), dma((ITERS, n_row)),
            dma((sums, n_col)), dma((sums, n_col)),
            dma((sums, n_row)), dma((sums, n_row)),
            dma((sums, n_col)), dma((sums, n_col)),
        ],
        compiler_params=pltpu.CompilerParams(
            collective_id=0, has_side_effects=True, vmem_limit_bytes=48 * 1024 * 1024
        ),
    )(table, blocks, start_block.T)
    return (
        basis.T,
        jnp.swapaxes(diag[:, :, :width], 1, 2),
        upper[:, :, :width],
    )


def solution(mesh):
    return jax.shard_map(
        per_device,
        mesh=mesh,
        in_specs=(
            P(("row", "col"), None, None),
            P(("row", "col"), None),
            P(("row", "col")),
            P(("row", "col"), None),
        ),
        out_specs=(P(("row", "col"), None), P(), P()),
        check_vma=False,
    )
```
